32 devices in a mesh: groups: 2 (over y), tile: 4 (over z), chan: 2 (over x), sub: 2 (over core).
Axes of the slice: x: 2, y: 2, z: 4, core: 2. Of those that a mesh axis runs over, the one named last changes fastest.
Arguments:
- activations: bfloat16 [256, 32, 256], P('chan', ('groups', 'tile'), 'sub'), parts along dimension 1, may hold values from -6 to 6
- out_grad: bfloat16 [256, 32, 256], P('chan', ('groups', 'tile'), 'sub'), parts along dimension 1, may hold values from -6 to 6
- weight: bfloat16 [256, 6912], P('chan'), may hold values from -0.078125 to 0.078125
Outputs:
- conv_out: bfloat16 [256, 32, 256], P('chan', ('groups', 'tile'), 'sub'), parts along dimension 1
- input_grad: bfloat16 [256, 32, 256], P('chan', ('groups', 'tile'), 'sub'), parts along dimension 1
- weight_grad: float32 [512, 6912], P(('groups', 'chan')), parts along dimension 0
The draws below stay inside these ranges and needn't reach their ends.
There are 2 independent parts, one for each index of `groups`. The reference program is written for one: setup_inputs(seed, part) draws one part's arguments, and reference() takes and returns one part's arrays. A program takes and returns all parts, laid end to end along the dimension named above; an argument that names none is the same for every part. Nothing has to cross between parts.
All inputs are finite; a program needn't handle non-finite values.
Results may differ from the reference program's by a relative error of at most 0.0034.
Values may be sent and summed in bfloat16 or wider, within the bound.
No kernel may reach another device: no remote copies, remote signals or barrier semaphores. Data moves between devices by JAX's collectives and lax.ppermute only.
A program may use at most 64 MiB of HBM per device.

```python
import math
import jax
import jax.numpy as jnp
from jax import lax

CH = 256
ZS = 4
NX = 16
NY = 64


def levels(own_key, extent, split, least, largest):
    factor_of = 1.0
    for dim, blocks in split:
        heights = jax.random.uniform(jax.random.fold_in(jax.random.fold_in(own_key, 6), dim), (blocks,), jnp.float32, least / len(split), largest / len(split))
        factor_of = factor_of * jnp.repeat(jnp.exp(heights), extent[dim] // blocks).reshape((-1,) + (1,) * (len(extent) - 1 - dim))
    return factor_of


def normal_values(rng, extent, width, bound, split=(), kind=jnp.bfloat16):
    array = width * jax.random.normal(rng, extent, jnp.float32)
    if split:
        array = array * levels(rng, extent, split, -0.22, 0.18)
    return jnp.clip(array, -bound, bound).astype(kind)


def setup_inputs(seed: int = 0, part: int = 0) -> dict:
    key_of = jax.random.split(jax.random.key(seed), 4)
    part_splits = jax.random.split(jax.random.fold_in(key_of[3], part), 4)
    return {
        "activations": normal_values(part_splits[0], (CH, NX, NY * ZS), 1.0, 6.0, ((0, 2), (1, 4), (2, 2))),
        "out_grad": normal_values(part_splits[1], (CH, NX, NY * ZS), 1.0, 6.0, ((0, 2), (1, 4), (2, 2))),
        "weight": normal_values(key_of[2], (CH, CH * 27), (CH * 27) ** -0.5, 0.078125, ((0, 2),)),
    }


def convolve(field, filt):
    return lax.conv_general_dilated(field, filt, (1, 1, 1), 'SAME', dimension_numbers=('NCDHW', 'OIDHW', 'NCDHW'), precision=lax.Precision.HIGHEST)

def reference(activations, out_grad, weight):
    channels = activations.shape[0]
    planes = activations.shape[1]
    rows_y = activations.shape[2] // ZS
    field = activations.astype(jnp.float32).reshape(1, channels, planes, rows_y, ZS)
    gradient = out_grad.astype(jnp.float32).reshape(1, channels, planes, rows_y, ZS)
    filt = weight.astype(jnp.float32).reshape(channels, channels, 3, 3, 3)
    output, backward = jax.vjp(convolve, field, filt)
    grad_field, grad_filt = backward(gradient)
    scale = 1.0 / math.sqrt(planes * rows_y * ZS)
    conv_out = output.reshape(activations.shape).astype(jnp.bfloat16)
    input_grad = grad_field.reshape(activations.shape).astype(jnp.bfloat16)
    weight_grad = (grad_filt * scale).reshape(channels, channels * 27).astype(jnp.float32)
    return (conv_out, input_grad, weight_grad)
```

```python
import functools
import math

import jax
import jax.numpy as jnp
from jax import lax
from jax.experimental import pallas as pl
from jax.experimental.pallas import tpu as pltpu
from jax.sharding import PartitionSpec as P

ZS = 4
BF = jnp.bfloat16
F32 = jnp.float32
VMEM = pl.BlockSpec(memory_space=pltpu.VMEM)
SMEM = pl.BlockSpec(memory_space=pltpu.SMEM)
PARAMS = pltpu.CompilerParams(vmem_limit_bytes=56 * 2**20)


def cost(flops, bytes_accessed):
    return pl.CostEstimate(flops=flops, bytes_accessed=bytes_accessed, transcendentals=0)


def rotate(x, axis, k):
    n = lax.axis_size(axis)
    if k % n == 0:
        return x
    return lax.ppermute(x, axis, [(i, (i + k) % n) for i in range(n)])


def shifted(v, dy, dz, sub, count):
    lanes = v.shape[-1]
    move = ZS * dy + dz
    if move == 0:
        return v
    turned = pltpu.roll(v, (-move) % lanes, v.ndim - 1)
    lane = lax.broadcasted_iota(jnp.int32, v.shape, v.ndim - 1)
    pos = lane + sub * (lanes // count)
    pos = jnp.where(pos >= lanes, pos - lanes, pos)
    z = pos & (ZS - 1)
    y = pos >> 2
    inside = (z + dz >= 0) & (z + dz < ZS) & (y + dy >= 0) & (y + dy < lanes // ZS)
    return jnp.where(inside, turned, jnp.zeros((), v.dtype))


def filter_kernel(n_chan, ids, w_ref, wt_ref, wn_ref, rows):
    local, columns = w_ref.shape
    total = columns // 27
    mine = ids[1]
    for j in range(columns // 128):
        rows[j * 128 : (j + 1) * 128, :] = w_ref[:, j * 128 : (j + 1) * 128].astype(F32).T
    for t in range(27):
        for j in range(n_chan):
            true = lax.rem(mine + j, n_chan)
            v = rows[pl.ds(true * (local * 27) + t, local, stride=27), :]
            wt_ref[j * local : (j + 1) * local, t * local : (t + 1) * local] = v.astype(BF)
            at = t * total + j * local
            wn_ref[:, at : at + local] = v.T.astype(BF)


def conv_kernel(n_chan, n_sub, n_tile, ids, *refs):
    n_act = 3 * n_chan * n_sub
    acts, grads = refs[:n_act], refs[n_act : n_act + 3 * n_sub]
    wt_ref, wn_ref = refs[n_act + 3 * n_sub : n_act + 3 * n_sub + 2]
    conv_ref = refs[n_act + 3 * n_sub + 2]
    part_refs = refs[n_act + 3 * n_sub + 3 : n_act + 3 * n_sub + 3 + n_chan]
    act_cols, grad_cols = refs[-2:]
    planes, local, span = acts[0].shape
    total = n_chan * local
    tile, sub = ids[0], ids[2]

    def plane(group, x):
        if x == 0:
            v = jnp.concatenate([r[planes - 1] for r in group[1]], axis=1)
            return jnp.where(tile > 0, v, jnp.zeros((), BF))
        if x == planes + 1:
            v = jnp.concatenate([r[0] for r in group[2]], axis=1)
            return jnp.where(tile < n_tile - 1, v, jnp.zeros((), BF))
        return jnp.concatenate([r[x - 1] for r in group[0]], axis=1)

    for j in range(n_chan):
        group = [[acts[(b * n_chan + j) * n_sub + u] for u in range(n_sub)] for b in range(3)]
        for x in range(planes + 2):
            v = plane(group, x)
            for bc in range(9):
                s = shifted(v, bc // 3 - 1, bc % 3 - 1, sub, n_sub)
                at = bc * total + j * local
                act_cols[at : at + local, x * span : (x + 1) * span] = s[:, :span]
    group = [[grads[b * n_sub + u] for u in range(n_sub)] for b in range(3)]
    for x in range(planes + 2):
        v = plane(group, x)
        for bc in range(9):
            s = shifted(v, 1 - bc // 3, 1 - bc % 3, sub, n_sub)
            grad_cols[bc * local : (bc + 1) * local, x * span : (x + 1) * span] = s[:, :span]
    cells = planes * span
    out = jnp.zeros((local, cells), F32)
    for a in range(3):
        out += jnp.dot(
            wn_ref[:, a * 9 * total : (a + 1) * 9 * total],
            act_cols[:, a * span : a * span + cells],
            preferred_element_type=F32,
        )
    for x in range(planes):
        conv_ref[:, x, :] = out[:, x * span : (x + 1) * span].astype(BF)
    for j in range(n_chan):
        part = jnp.zeros((local, cells), F32)
        for a in range(3):
            part += jnp.dot(
                wt_ref[j * local : (j + 1) * local, a * 9 * local : (a + 1) * 9 * local],
                grad_cols[:, (2 - a) * span : (2 - a) * span + cells],
                preferred_element_type=F32,
            )
        part_refs[j][...] = part


def update_kernel(n_chan, n_sub, n_tile, scale, ids, *refs):
    n_act = n_tile * n_chan * n_sub
    acts, grads = refs[:n_act], refs[n_act : n_act + n_tile * n_sub]
    parts = refs[n_act + n_tile * n_sub : n_act + n_tile * n_sub + n_chan]
    out_ref, ig_ref, act_all, grad_all, rows = refs[-5:]
    planes, local, span = acts[0].shape
    wide = span * n_sub
    depth = n_tile * planes * wide
    total = n_chan * local
    tile, mine, sub = ids[0], ids[1], ids[2]
    act_all[:, :wide] = jnp.zeros((total, wide), BF)
    act_all[:, depth + wide :] = jnp.zeros((total, wide), BF)
    for k in range(n_tile):
        first = lax.rem(tile - k + n_tile, n_tile) * planes
        for x in range(planes):
            at = pl.multiple_of((first + x) * wide, wide)
            for j in range(n_chan):
                for u in range(n_sub):
                    act_all[
                        j * local : (j + 1) * local,
                        pl.ds(pl.multiple_of(at + wide + u * span, span), span),
                    ] = acts[(k * n_chan + j) * n_sub + u][x]
            v = jnp.concatenate([grads[k * n_sub + u][x] for u in range(n_sub)], axis=1)
            for bc in range(9):
                grad_all[bc * local : (bc + 1) * local, pl.ds(at, wide)] = shifted(
                    v, 1 - bc // 3, 1 - bc % 3, sub, n_sub
                )
    ig = parts[0][...]
    for j in range(1, n_chan):
        ig = ig + parts[j][...]
    for x in range(planes):
        ig_ref[:, x, :] = ig[:, x * span : (x + 1) * span].astype(BF)
    group = max(1, 256 // local)

    def taps(a, carry):
        lhs = act_all[:, pl.ds(pl.multiple_of(a * wide, wide), depth)]
        for p in range(0, 9, group):
            n = min(group, 9 - p)
            r = lax.dot_general(
                lhs,
                grad_all[p * local : (p + n) * local, :],
                (((1,), (1,)), ((), ())),
                preferred_element_type=F32,
            )
            for i in range(n):
                for j in range(n_chan):
                    true = lax.rem(mine + j, n_chan)
                    start = true * (local * 27) + a * 9 + p + i
                    rows[pl.ds(start, local, stride=27), :] = r[
                        j * local : (j + 1) * local, i * local : (i + 1) * local
                    ]
        return carry

    lax.fori_loop(0, 3, taps, 0)
    for j in range(total * 27 // 128):
        out_ref[:, j * 128 : (j + 1) * 128] = rows[j * 128 : (j + 1) * 128, :].T * scale


def body(activations, out_grad, weight):
    local, planes, span = activations.shape
    n_tile, n_chan, n_sub = (lax.axis_size(a) for a in ("tile", "chan", "sub"))
    total = weight.shape[1] // 27
    cells = planes * span
    scale = 1.0 / math.sqrt(cells * n_tile * n_sub)
    ids = jnp.stack([lax.axis_index(a) for a in ("tile", "chan", "sub")]).astype(jnp.int32)
    act = activations.transpose(1, 0, 2)
    grad = out_grad.transpose(1, 0, 2)
    order = [0, 1, n_tile - 1] + list(range(2, n_tile - 1))
    acts = {k: rotate(act, "tile", k) for k in order}
    grads = {k: rotate(grad, "tile", k) for k in order}
    acts = {(k, j): rotate(acts[k], "chan", -j) for k in order for j in range(n_chan)}
    acts = {(k, j, u): rotate(acts[k, j], "sub", -u) for k, j in acts for u in range(n_sub)}
    grads = {(k, u): rotate(grads[k], "sub", -u) for k in order for u in range(n_sub)}

    wt, wn = pl.pallas_call(
        functools.partial(filter_kernel, n_chan),
        out_shape=(
            jax.ShapeDtypeStruct((total, 27 * local), BF),
            jax.ShapeDtypeStruct((local, 27 * total), BF),
        ),
        in_specs=[SMEM, VMEM],
        out_specs=(VMEM, VMEM),
        scratch_shapes=[pltpu.VMEM((total * 27, local), F32)],
        compiler_params=PARAMS,
        cost_estimate=cost(0, 12 * local * total * 27),
    )(ids, weight)

    near = order[:3]
    conv_in = [acts[k, j, u] for k in near for j in range(n_chan) for u in range(n_sub)]
    conv_in += [grads[k, u] for k in near for u in range(n_sub)]
    conv_out, *parts = pl.pallas_call(
        functools.partial(conv_kernel, n_chan, n_sub, n_tile),
        out_shape=[jax.ShapeDtypeStruct((local, planes, span), BF)]
        + [jax.ShapeDtypeStruct((local, cells), F32)] * n_chan,
        in_specs=[SMEM] + [VMEM] * (len(conv_in) + 2),
        out_specs=[VMEM] * (n_chan + 1),
        scratch_shapes=[
            pltpu.VMEM((9 * total, (planes + 2) * span), BF),
            pltpu.VMEM((9 * local, (planes + 2) * span), BF),
        ],
        compiler_params=PARAMS,
        cost_estimate=cost(4 * 27 * local * total * cells, 4 * 2**20),
    )(ids, *conv_in, wt, wn)
    parts = [rotate(part, "chan", j) for j, part in enumerate(parts)]

    update_in = [acts[k, j, u] for k in range(n_tile) for j in range(n_chan) for u in range(n_sub)]
    update_in += [grads[k, u] for k in range(n_tile) for u in range(n_sub)]
    depth = n_tile * planes * span * n_sub
    weight_grad, input_grad = pl.pallas_call(
        functools.partial(update_kernel, n_chan, n_sub, n_tile, scale),
        out_shape=(
            jax.ShapeDtypeStruct((local, total * 27), F32),
            jax.ShapeDtypeStruct((local, planes, span), BF),
        ),
        in_specs=[SMEM] + [VMEM] * (len(update_in) + n_chan),
        out_specs=(VMEM, VMEM),
        scratch_shapes=[
            pltpu.VMEM((total, depth + 2 * span * n_sub), BF),
            pltpu.VMEM((9 * local, depth), BF),
            pltpu.VMEM((total * 27, local), F32),
        ],
        compiler_params=PARAMS,
        cost_estimate=cost(2 * 27 * local * total * depth, 8 * 2**20),
    )(ids, *update_in, *parts)
    return conv_out, input_grad, weight_grad


def solution(mesh):
    placed = (
        P("chan", ("groups", "tile"), "sub"),
        P("chan", ("groups", "tile"), "sub"),
        P("chan", None),
    )
    return jax.shard_map(
        body,
        mesh=mesh,
        in_specs=placed,
        out_specs=(
            P("chan", ("groups", "tile"), "sub"),
            P("chan", ("groups", "tile"), "sub"),
            P(("groups", "chan"), None),
        ),
        check_vma=False,
    )
```

```python
import functools
import math

import jax
import jax.numpy as jnp
from jax import lax
from jax.experimental import pallas as pl
from jax.experimental.pallas import tpu as pltpu
from jax.sharding import PartitionSpec as P

ZS = 4
BF = jnp.bfloat16
F32 = jnp.float32
VMEM = pl.BlockSpec(memory_space=pltpu.VMEM)
SMEM = pl.BlockSpec(memory_space=pltpu.SMEM)
HBM = pl.BlockSpec(memory_space=pltpu.HBM)
MIB = 2**20
TINY = pl.CostEstimate(flops=1000, bytes_accessed=1000, transcendentals=0)


def params(mib):
    return pltpu.CompilerParams(vmem_limit_bytes=mib * MIB)


def shape(dims, dtype):
    return jax.ShapeDtypeStruct(dims, dtype)


def swap(x, axis, k):
    return lax.ppermute(x, axis, [(i, i ^ k) for i in range(lax.axis_size(axis))])


def rotate(x, axis, k):
    n = lax.axis_size(axis)
    if k % n == 0:
        return x
    return lax.ppermute(x, axis, [(i, (i + k) % n) for i in range(n)])


def after(*values):
    return lax.optimization_barrier(values)


def y_inside(lanes, dy, sub, count):
    lane = lax.broadcasted_iota(jnp.int32, (16, lanes), 1)
    pos = lane + sub * (lanes // count)
    pos = jnp.where(pos >= lanes, pos - lanes, pos) + ZS * dy
    return jnp.where((pos >= 0) & (pos < lanes), 1.0, 0.0).astype(BF)


def z_inside(lanes, dz, dtype):
    z = (lax.broadcasted_iota(jnp.int32, (16, lanes), 1) & (ZS - 1)) + dz
    return jnp.where((z >= 0) & (z < ZS), 1.0, 0.0).astype(dtype)


def moved(v, step, mask):
    if step == 0:
        return v
    lanes = v.shape[-1]
    turned = pltpu.roll(v, (-step) % lanes, v.ndim - 1)
    return turned * mask[:1]


def pack_kernel(act_ref, grad_ref, a_ref, g_ref, both_ref):
    planes = act_ref.shape[1]
    for x in range(planes):
        a = act_ref[:, x, :]
        g = grad_ref[:, x, :]
        a_ref[x] = a
        g_ref[x] = g
        both_ref[x] = a
        both_ref[planes + x] = g


def pack(activations, out_grad):
    local, planes, span = activations.shape
    one = shape((planes, local, span), BF)
    return pl.pallas_call(
        pack_kernel,
        out_shape=(one, one, shape((2 * planes, local, span), BF)),
        in_specs=[VMEM] * 2,
        out_specs=(VMEM,) * 3,
        compiler_params=params(8),
        cost_estimate=TINY,
    )(activations, out_grad)


def halves_kernel(count, *refs):
    for n in range(count):
        rows = refs[n].shape[0] // 2
        for half in range(2):
            refs[count + 2 * n + half][...] = refs[n][half * rows : (half + 1) * rows]


def halves(*arrays):
    outs = []
    for a in arrays:
        outs += [shape((a.shape[0] // 2,) + a.shape[1:], BF)] * 2
    return pl.pallas_call(
        functools.partial(halves_kernel, len(arrays)),
        out_shape=outs,
        in_specs=[VMEM] * len(arrays),
        out_specs=[VMEM] * len(outs),
        compiler_params=params(8),
        cost_estimate=TINY,
    )(*arrays)


def list_of(blocks):
    return {name: n for n, name in enumerate(blocks)}


def filter_kernel(n_chan, ids, w_ref, wt_ref, wn_ref, rows):
    local, columns = w_ref.shape
    total = columns // 27
    mine = ids[1]
    for at in range(0, columns, 128):
        rows[at : at + 128, :] = w_ref[:, at : at + 128].astype(F32).T
    for t in range(27):
        ab, c = t // 3, t % 3
        for j in range(n_chan):
            true = lax.rem(mine + j, n_chan)
            v = rows[pl.ds(true * (local * 27) + t, local, stride=27), :]
            row = (j * 3 + c) * local
            wt_ref[row : row + local, ab * local : (ab + 1) * local] = v.astype(BF)
            at = ab * total + j * local
            wn_ref[c * local : (c + 1) * local, at : at + local] = v.T.astype(BF)


def arrange_filter(ids, weight, n_chan):
    local, columns = weight.shape
    total = columns // 27
    return pl.pallas_call(
        functools.partial(filter_kernel, n_chan),
        out_shape=(shape((3 * total, 9 * local), BF), shape((3 * local, 9 * total), BF)),
        in_specs=[SMEM, VMEM],
        out_specs=(VMEM, VMEM),
        scratch_shapes=[pltpu.VMEM((columns, local), F32)],
        compiler_params=params(16),
        cost_estimate=TINY,
    )(ids, weight)


def z_taps(v, rows, cells, direction):
    out = v[rows : 2 * rows]
    for c in (0, 2):
        dz = direction * (c - 1)
        mask = z_inside(cells, dz, F32)
        out = out + moved(v[c * rows : (c + 1) * rows], dz, mask)
    return out


def edge_planes(refs, layout, sizes, near, tile):
    n_tile, _, n_sub = sizes

    def row(key, slot, x):
        return jnp.concatenate([refs[layout[key + (slot, u)]][x] for u in range(n_sub)], axis=1)

    def plane(key, x, planes):
        if 0 < x <= planes:
            return row(key, 0, x - 1)
        beyond = x > planes
        even, odd = near[beyond]
        at = 0 if beyond else planes - 1
        v = row(key, even, at)
        if odd != even:
            v = jnp.where((tile & 1) == 1, row(key, odd, at), v)
        inside = tile < n_tile - 1 if beyond else tile > 0
        return jnp.where(inside, v, jnp.zeros((), BF))

    return plane


def conv_kernel(sizes, layout, near, ids, *refs):
    *arrays, wn_ref, conv_ref, act_cols = refs
    _, n_chan, n_sub = sizes
    local, planes, span = conv_ref.shape
    total = n_chan * local
    cells = planes * span
    plane = edge_planes(arrays, layout, sizes, near, ids[0])
    masks = [y_inside(span * n_sub, dy, ids[2], n_sub) for dy in (-1, 0, 1)]
    for x in range(planes + 2):
        for j in range(n_chan):
            v = plane(("act", j), x, planes)
            for b in range(3):
                s = moved(v, ZS * (b - 1), masks[b])
                at = b * total + j * local
                act_cols[at : at + local, x * span : (x + 1) * span] = s[:, :span]
    out = jnp.zeros((3 * local, cells), F32)
    for a in range(3):
        out += jnp.dot(
            wn_ref[:, a * 3 * total : (a + 1) * 3 * total],
            act_cols[:, a * span : a * span + cells],
            preferred_element_type=F32,
        )
    out = z_taps(out, local, cells, 1)
    for x in range(planes):
        conv_ref[:, x, :] = out[:, x * span : (x + 1) * span].astype(BF)


def convolve(ids, blocks, wn, near, sizes, block):
    local, planes, span = block
    arrays = list(blocks.values())
    return pl.pallas_call(
        functools.partial(conv_kernel, sizes, list_of(blocks), near),
        out_shape=shape(block, BF),
        in_specs=[SMEM] + [VMEM] * (len(arrays) + 1),
        out_specs=VMEM,
        scratch_shapes=[pltpu.VMEM((3 * sizes[1] * local, (planes + 2) * span), BF)],
        compiler_params=params(16),
        cost_estimate=TINY,
    )(ids, *arrays, wn)


def terms_kernel(sizes, layout, near, ids, *refs):
    _, n_chan, n_sub = sizes
    arrays, wt_ref = refs[: -2 - n_chan], refs[-2 - n_chan]
    part_refs, grad_cols = refs[-1 - n_chan : -1], refs[-1]
    _, local, span = arrays[0].shape
    cells = part_refs[0].shape[1]
    planes = cells // span
    plane = edge_planes(arrays, layout, sizes, near, ids[0])
    masks = [y_inside(span * n_sub, dy, ids[2], n_sub) for dy in (-1, 0, 1)]
    for x in range(planes + 2):
        v = plane(("grad",), x, planes)
        for b in range(3):
            s = moved(v, ZS * (1 - b), masks[2 - b])
            grad_cols[b * local : (b + 1) * local, x * span : (x + 1) * span] = s[:, :span]
    for j in reversed(range(n_chan)):
        part = jnp.zeros((3 * local, cells), F32)
        for a in range(3):
            part += jnp.dot(
                wt_ref[j * 3 * local : (j + 1) * 3 * local, a * 3 * local : (a + 1) * 3 * local],
                grad_cols[:, (2 - a) * span : (2 - a) * span + cells],
                preferred_element_type=F32,
            )
        part_refs[j][...] = z_taps(part, local, cells, -1)


def input_terms(ids, blocks, wt, near, sizes, block):
    local, planes, span = block
    n_chan = sizes[1]
    arrays = list(blocks.values())
    return pl.pallas_call(
        functools.partial(terms_kernel, sizes, list_of(blocks), near),
        out_shape=[shape((local, planes * span), F32)] * n_chan,
        in_specs=[SMEM] + [VMEM] * (len(arrays) + 1),
        out_specs=[VMEM] * n_chan,
        scratch_shapes=[pltpu.VMEM((3 * local, (planes + 2) * span), BF)],
        compiler_params=params(16),
        cost_estimate=TINY,
    )(ids, *arrays, wt)


def update_kernel(sizes, block, layout, count, runs, earlier, final, scale, ids, *refs):
    n_tile, n_chan, n_sub = sizes
    local, planes, span = block
    wide = span * n_sub
    total = n_chan * local
    refs = list(refs)
    arrays = [refs.pop(0) for _ in range(count)]
    edges = [(refs.pop(0), refs.pop(0)) for _ in earlier]
    acc_in = refs.pop(0) if earlier else None
    parts = [refs.pop(0) for _ in range(n_chan)] if final else []
    outs = [refs.pop(0) for _ in range(2 if final else 2 * len(runs) + 1)]
    windows = [(refs.pop(0), refs.pop(0)) for _ in runs]
    rows, out_vmem, sems = refs if final else (None,) * 3
    mine, sub = ids[1], ids[2]
    ymask = [y_inside(wide, dy, sub, n_sub) for dy in (-1, 0, 1)]
    zmask = [z_inside(wide, dz, BF) for dz in (-1, 0, 1)]

    def row(key, slot, x):
        return jnp.concatenate([arrays[layout[key + (slot, u)]][x] for u in range(n_sub)], axis=1)

    known = []
    for (act_edge, grad_edge), (place, length) in zip(edges, earlier, strict=True):
        ends = [(lambda n=n, e=e: e[n]) for e in (act_edge, grad_edge) for n in range(2)]
        known.append((ids[3 + place], length, ends))
    spans = []
    for (act_win, grad_win), slots in zip(windows, runs, strict=True):
        start = ids[3 + slots[0][1]]
        long = len(slots) * planes
        for place, _, slot in slots:
            for x in range(planes):
                at = (x + 1) * wide
                if len(slots) > 1:
                    at = pl.multiple_of((ids[3 + place] - start) * (planes * wide) + at, wide)
                for j in range(n_chan):
                    v = row(("act", j), slot, x)
                    for b in range(3):
                        top = b * total + j * local
                        act_win[top : top + local, pl.ds(at, wide)] = moved(
                            v, ZS * (b - 1), ymask[b]
                        )
                v = row(("grad",), slot, x)
                for c in range(3):
                    grad_win[c * local : (c + 1) * local, pl.ds(at, wide)] = moved(
                        v, 1 - c, zmask[2 - c]
                    )
        if known:
            low, high = slice(0, wide), slice((long + 1) * wide, (long + 2) * wide)
            for win in (act_win, grad_win):
                for side in (low, high):
                    win[:, side] = jnp.zeros((win.shape[0], wide), BF)
            for begin, length, ends in known:

                @pl.when(begin + length == start)
                def _():
                    act_win[:, low] = ends[1]()
                    grad_win[:, low] = ends[3]()

                @pl.when(begin == start + len(slots))
                def _():
                    act_win[:, high] = ends[0]()
                    grad_win[:, high] = ends[2]()

        if known:
            spans.append([(1, long + 1), (1, long), (0, long)])
        else:
            spans.append([(2, long), (1, long), (1, long - 1)])
        sides = [slice(wide, 2 * wide), slice(long * wide, (long + 1) * wide)]
        ends = [(lambda w=w, s=s: w[:, s]) for w in (act_win, grad_win) for s in sides]
        known.append((start, len(slots), ends))
        if not final:
            n = 2 * (len(spans) - 1)
            for side in range(2):
                outs[n][side] = ends[side]()
                outs[n + 1][side] = ends[2 + side]()

    if final:
        out_ref, ig_ref = outs
        ig = parts[0][...]
        for j in range(1, n_chan):
            ig = ig + parts[j][...]
        for x in range(planes):
            ig_ref[:, x, :] = ig[:, x * span : (x + 1) * span].astype(BF)

    for a in range(3):
        for b in range(3):
            r = acc_in[a * 3 + b] if earlier else None
            for (act_win, grad_win), ranges in zip(windows, spans, strict=True):
                first, last = ranges[a]
                d = lax.dot_general(
                    grad_win[:, first * wide : (last + 1) * wide],
                    act_win[
                        b * total : (b + 1) * total, (first + a - 1) * wide : (last + a) * wide
                    ],
                    (((1,), (1,)), ((), ())),
                    preferred_element_type=F32,
                )
                r = d if r is None else r + d
            if not final:
                outs[-1][a * 3 + b] = r
                continue
            for c in range(3):
                for j in range(n_chan):
                    true = lax.rem(mine + j, n_chan)
                    at = true * (local * 27) + a * 9 + b * 3 + c
                    tap = r[c * local : (c + 1) * local, j * local : (j + 1) * local]
                    rows[pl.ds(at, local, stride=27), :] = tap.T
    if final:
        copies = []
        width = total * 27 // sems.shape[0]
        for n in range(sems.shape[0]):
            for at in range(n * width, (n + 1) * width, 128):
                out_vmem[:, at : at + 128] = rows[at : at + 128, :].T * scale
            some = slice(n * width, (n + 1) * width)
            copies.append(pltpu.make_async_copy(out_vmem.at[:, some], out_ref.at[:, some], sems.at[n]))
            copies[-1].start()
        for copy in copies:
            copy.wait()


def update(ids, blocks, runs, earlier, carried, parts, scale, sizes, block):
    n_tile, n_chan, n_sub = sizes
    local, planes, span = block
    wide = span * n_sub
    total = n_chan * local
    final = parts is not None
    arrays = list(blocks.values())
    extra = list(carried) + list(parts or [])
    if final:
        outs = [shape((local, total * 27), F32), shape(block, BF)]
    else:
        outs = [shape((2, 3 * n, wide), BF) for _ in runs for n in (total, local)]
        outs.append(shape((9, 3 * local, total), F32))
    scratch = [
        pltpu.VMEM((3 * n, (len(slots) * planes + 2) * wide), BF)
        for slots in runs
        for n in (total, local)
    ]
    if final:
        scratch.append(pltpu.VMEM((total * 27, local), F32))
        scratch.append(pltpu.VMEM((local, total * 27), F32))
        scratch.append(pltpu.SemaphoreType.DMA((3,)))
    return pl.pallas_call(
        functools.partial(
            update_kernel,
            sizes,
            block,
            list_of(blocks),
            len(arrays),
            runs,
            earlier,
            final,
            scale,
        ),
        out_shape=outs,
        in_specs=[SMEM] + [VMEM] * (len(arrays) + len(extra)),
        out_specs=[HBM, VMEM] if final else [VMEM] * len(outs),
        scratch_shapes=scratch,
        compiler_params=params(28 if n_tile == 4 else 58),
        cost_estimate=TINY,
    )(ids, *arrays, *extra)


def body(activations, out_grad, weight):
    block = local, planes, span = activations.shape
    sizes = n_tile, n_chan, n_sub = tuple(lax.axis_size(a) for a in ("tile", "chan", "sub"))
    scale = 1.0 / math.sqrt(planes * span * n_tile * n_sub)
    tile, chan, sub = (lax.axis_index(a) for a in ("tile", "chan", "sub"))
    paired = n_tile == 4
    if paired:
        places = [tile, tile ^ 1, tile ^ 2, tile ^ 3, tile & 2]
    else:
        places = [lax.rem(tile - k + n_tile, n_tile) for k in range(n_tile)] + [0 * tile]
    ids = jnp.stack([tile, chan, sub] + places).astype(jnp.int32)
    chans, subs = range(n_chan), range(n_sub)

    act, grad, both = pack(activations, out_grad)
    blocks = {}

    def share(v, *name):
        for u in subs:
            blocks[name + (u,)] = rotate(v, "sub", -u)

    def only(slots, kind=None):
        return {k: v for k, v in blocks.items() if k[-2] in slots and kind in (None, k[0])}

    def add(runs, earlier, carried, parts=None):
        used = only({slot for slots in runs for _, _, slot in slots})
        return update(ids, used, runs, earlier, carried, parts, scale, sizes, block)

    if not paired:
        wt, wn = arrange_filter(ids, weight, n_chan)
        for k in range(n_tile):
            a, g = rotate(act, "tile", k), rotate(grad, "tile", k)
            share(g, "grad", k)
            for j in chans:
                share(rotate(a, "chan", -j), "act", j, k)
        near = ((1, 1), (n_tile - 1, n_tile - 1))
        close = {0, 1, n_tile - 1}
        conv_out = convolve(ids, only(close, "act"), wn, near, sizes, block)
        parts = input_terms(ids, only(close, "grad"), wt, near, sizes, block)
        parts = [rotate(part, "chan", j) for j, part in enumerate(parts)]
        runs = (tuple((k, n_tile, k) for k in range(n_tile)),)
        weight_grad, input_grad = add(runs, (), (), parts)
        return conv_out, input_grad, weight_grad

    near = ((3, 1), (1, 3))
    first = swap(both, "tile", 1)
    third = swap(both, "tile", 3)
    wt, wn = arrange_filter(ids, weight, n_chan)
    for j in chans:
        share(rotate(act, "chan", -j), "act", j, 0)
    share(grad, "grad", 0)
    act_0, grad_0, acc = add((((0, 0, 0),),), (), ())
    first, third, wt, wn, acc = after(first, third, wt, wn, acc)
    far = swap(after(both, third)[0], "tile", 2)
    act_1, grad_1, act_3, grad_3 = halves(first, third)
    beside = [rotate(v, "chan", -j) for j in chans[1:] for v in (act_1, act_3)]
    share(grad_1, "grad", 1)
    share(grad_3, "grad", 3)
    share(act_1, "act", 0, 1)
    share(act_3, "act", 0, 3)
    parts = input_terms(ids, only({0, 1, 3}, "grad"), wt, near, sizes, block)
    tail = after(*beside, *parts)
    beside, parts = tail[: len(beside)], tail[len(beside) :]
    parts = [rotate(part, "chan", j) for j, part in enumerate(parts)]
    for n, v in enumerate(beside):
        share(v, "act", 1 + n // 2, (1, 3)[n % 2])
    runs = (((1, 1, 1),), ((3, 3, 3),))
    *edges, acc = add(runs, ((0, 1),), (act_0, grad_0, acc))
    far, acc, wn, *parts = after(far, acc, wn, *parts)
    act_2, grad_2 = halves(far)
    beside = [rotate(act_2, "chan", -j) for j in chans[1:]]
    conv_out = convolve(ids, only({0, 1, 3}, "act"), wn, near, sizes, block)
    conv_out, act_2, grad_2, *beside = after(conv_out, act_2, grad_2, *beside)
    share(act_2, "act", 0, 2)
    share(grad_2, "grad", 2)
    for j, v in enumerate(beside, 1):
        share(v, "act", j, 2)
    runs, earlier = (((2, 2, 2),),), ((0, 1), (1, 1), (3, 1))
    weight_grad, input_grad = add(runs, earlier, (act_0, grad_0, *edges, acc), parts)
    return conv_out, input_grad, weight_grad


def solution(mesh):
    placed = (
        P("chan", ("groups", "tile"), "sub"),
        P("chan", ("groups", "tile"), "sub"),
        P("chan", None),
    )
    return jax.shard_map(
        body,
        mesh=mesh,
        in_specs=placed,
        out_specs=(
            P("chan", ("groups", "tile"), "sub"),
            P("chan", ("groups", "tile"), "sub"),
            P(("groups", "chan"), None),
        ),
        check_vma=False,
    )
```
